32 devices in a mesh: dp: 8 (over y, x, core), shard: 4 (over z).
Axes of the slice: x: 2, y: 2, z: 4, core: 2. Of those that a mesh axis runs over, the one named last changes fastest.
Arguments:
- hidden_in: bfloat16 [4, 1024, 8192], P('shard', 'dp'), may hold values from -600 to 600
- norm_gain: bfloat16 [8192], replicated, may hold values from 0.5 to 1.5
- key_weight: bfloat16 [8192, 512], P('shard'), may hold values from -0.0625 to 0.0625
- queries: bfloat16 [4, 1024, 4096], P('shard', 'dp'), may hold values from -100 to 100
- logp_grad: bfloat16 [4, 1024, 4096], P('shard', 'dp'), may hold values from -6 to 6
- values: bfloat16 [4, 1024, 512], P('shard', 'dp'), may hold values from -6 to 6
- advantages: float32 [4, 1024], P('shard', 'dp'), may hold values from -4 to 4
- log_ratio: float32 [4, 1024], P('shard', 'dp'), may hold values from -0.5 to 0.5
- resp_lengths: int32 [4, 8], P('shard'), may hold values from 1 to 512, 1024 in all within a row
- block_slots: int32 [4, 64], P('shard', 'dp'), may hold values from 0 to 63, as said below
Outputs:
- input_grad: bfloat16 [4, 1024, 8192], P('shard', 'dp')
- query_grad: bfloat16 [4, 1024, 4096], P('shard', 'dp')
- value_grad: bfloat16 [4, 1024, 512], P('shard', 'dp')
- key_weight_grad: float32 [8, 8192, 512], P('dp', 'shard')
- gain_grad: float32 [8, 8192], P('dp', 'shard')
The draws below stay inside these ranges and needn't reach their ends.
Inputs may be any that keep to these rules, and one draw needn't show every extreme that they name: `resp_lengths`: row g lists the response lengths of stream g; they sum to 1024 and the longest is 512. `block_slots`: each row is a permutation of the 64 slots; slot // 8 is the index along dp whose balanced rows take the block. The 8 blocks of the rows of one device go to 8 different indices along dp, so one device sends at most one block to another.
All inputs are finite; a program needn't handle non-finite values.
Results may differ from the reference program's by a relative error of at most 0.025.
The reference program's roundings to bfloat16 on the way count: a program that leaves them out, or rounds other values in their place, can miss the bound.
Values may be sent and summed in bfloat16 or wider, within the bound.
A program may use at most 128 MiB of HBM per device.

```python
import math
import jax
import jax.numpy as jnp
import numpy as np
from jax import lax

D = 8192
HD = 128
QH = 32
KVH = 4
TOK_DEV = 128
BPD = 8
NRESP = 8
STREAMS = 4
STREAM = 1024
LMAX = 512
BLK = 16
NBLK = 64
N_DP = 8


def draw_hidden_in(key, part):
    key = jax.random.fold_in(key, 11)
    first = jax.random.fold_in(key, 0)
    base = jax.random.truncated_normal(first, -4.0, 4.0, (STREAMS, STREAM, D), jnp.float32)
    return base.astype(jnp.bfloat16)


def draw_queries(key, part):
    key = jax.random.fold_in(key, 23)
    first = jax.random.fold_in(key, 0)
    base = jax.random.truncated_normal(first, -4.0, 4.0, (STREAMS, STREAM, QH * HD), jnp.float32)
    return base.astype(jnp.bfloat16)


def slot_order(key):
    return jax.random.permutation(key, BPD)


def table_for_stream(key):
    devices = NBLK // BPD
    first, second, third, fourth = jax.random.split(key, 4)
    relabel = jax.random.permutation(first, devices)
    shifted = jax.random.permutation(second, devices)
    offsets = jax.random.permutation(third, devices)[:BPD]
    target = relabel[(shifted[:, None] + offsets[None, :]) % devices]
    within = jax.vmap(slot_order)(jax.random.split(fourth, devices))
    place = within[target, jnp.arange(BPD)[None, :]]
    return (target * BPD + place).reshape(NBLK).astype(jnp.int32)


def draw_block_slots(key, part):
    key = jax.random.fold_in(key, 37)
    return jax.vmap(table_for_stream)(jax.random.split(key, STREAMS))


def shard_levels(key, extent, cuts, low, largest):
    def one(dim, shards_of):
        draws = jax.random.uniform(jax.random.fold_in(jax.random.fold_in(key, 6), dim), (shards_of,), jnp.float32, low / len(cuts), largest / len(cuts))
        return jnp.repeat(jnp.exp(draws), extent[dim] // shards_of).reshape((-1,) + (1,) * (len(extent) - dim - 1))

    gain = one(*cuts[0])
    for cut in cuts[1:]:
        gain = gain * one(*cut)
    return gain


def length_profile(count, total, limit, slope):
    loads = [(1 << 20) // math.isqrt(standing ** slope) + 1 for standing in range(2, count + 1)]
    surplus, counts = total - limit - (count - 1), [1] * (count - 1)
    while surplus > 0:
        movable = [i for i in range(count - 1) if counts[i] < limit]
        pool, remaining = sum([loads[i] for i in movable]), surplus
        for i in movable:
            more = min(limit - counts[i], max(1, remaining * loads[i] // pool), surplus)
            counts[i] = counts[i] + more
            surplus = surplus - more
    return np.array([limit] + counts)


def uneven_parts(key, number_of, total, reach, lean):
    if number_of == 2:
        one = jax.random.randint(key, (), max(1, total - reach), min(reach, total - 1) + 1)
        return jnp.stack([one, total - one])
    sizes = jnp.asarray(length_profile(number_of, total, reach, lean), jnp.int32)
    couples = (number_of - 1) // 2
    source_of, sink = sizes[1:1 + 2 * couples:2], sizes[2:2 + 2 * couples:2]
    room = jnp.minimum(source_of - 1, reach - sink)
    moved = jax.random.randint(jax.random.fold_in(key, 1), (couples,), 0, 1 << 20) % (room + 1)
    sizes = sizes.at[1:1 + 2 * couples:2].set(source_of - moved).at[2:2 + 2 * couples:2].set(sink + moved)
    return sizes[jax.random.permutation(jax.random.fold_in(key, 2), number_of)]


def centred(stream_key, shape, spread, most, pieces=(), held_as=jnp.bfloat16):
    level = shard_levels(stream_key, shape, pieces, -0.22, 0.18) if pieces else 1.0
    result = jax.random.normal(stream_key, shape, jnp.float32) * spread * level
    return jnp.minimum(jnp.maximum(result, -most), most).astype(held_as)


def setup_inputs(seed: int = 0) -> dict:
    splits = jax.random.split(jax.random.key(seed), 11)
    hidden_in = draw_hidden_in(jax.random.fold_in(splits[10], 71), 0)
    norm_gain = jnp.clip(1.0 + 0.1 * jax.random.normal(splits[1], (D,), jnp.float32), 0.5, 1.5).astype(jnp.bfloat16)
    key_weight = centred(splits[2], (D, KVH * HD), D ** -0.5, 0.0625, ((0, 4),))
    queries = draw_queries(jax.random.fold_in(splits[10], 71), 0)
    logp_grad = centred(splits[4], (STREAMS, STREAM, QH * HD), 1.0, 6.0, ((0, 4), (1, 8)))
    values = centred(splits[5], (STREAMS, STREAM, KVH * HD), 1.0, 6.0, ((0, 4), (1, 8)))
    advantages = centred(splits[6], (STREAMS, STREAM), 1.0, 4.0, ((0, 4), (1, 8)), jnp.float32)
    log_ratio = jnp.clip(jax.random.uniform(splits[7], (STREAMS, STREAM), jnp.float32, -0.5, 0.5) * shard_levels(splits[7], (STREAMS, STREAM), ((0, 4), (1, 8)), -0.4, 0.0), -0.5, 0.5)
    resp_lengths = jax.vmap(lambda own: uneven_parts(own, NRESP, STREAM, LMAX, 2))(jax.random.split(splits[8], STREAMS)).reshape((STREAMS, NRESP)).astype(jnp.int32)
    block_slots = draw_block_slots(jax.random.fold_in(splits[10], 71), 0)
    return dict(hidden_in=hidden_in, norm_gain=norm_gain, key_weight=key_weight, queries=queries, logp_grad=logp_grad, values=values, advantages=advantages, log_ratio=log_ratio, resp_lengths=resp_lengths, block_slots=block_slots)


norm_eps = 1e-05
rope_base = 500000.0
upper_log = math.log(1.2)
lower_log = math.log(0.8)
masked_score = -1e+30

def rope_tables(positions, head_size):
    half_size = head_size // 2
    frequency = rope_base ** (-(jnp.arange(half_size, dtype=jnp.float32) * 2.0) / head_size)
    angles = positions.astype(jnp.float32)[:, None] * frequency[None, :]
    return (jnp.cos(angles)[:, None, :], jnp.sin(angles)[:, None, :])

def rotate(tensor, cosine_table, sine_table):
    half_size = tensor.shape[-1] // 2
    first_half = tensor[..., :half_size]
    second_half = tensor[..., half_size:]
    return jnp.concatenate([first_half * cosine_table - second_half * sine_table, second_half * cosine_table + first_half * sine_table], axis=-1)

def rotate_back(tensor, cosine_table, sine_table):
    half_size = tensor.shape[-1] // 2
    first_half = tensor[..., :half_size]
    second_half = tensor[..., half_size:]
    return jnp.concatenate([first_half * cosine_table + second_half * sine_table, second_half * cosine_table - first_half * sine_table], axis=-1)

def segment_info(lengths, row_ids):
    seg_ends = jnp.cumsum(lengths).astype(jnp.int32)
    starts = (seg_ends - lengths).astype(jnp.int32)
    inside = (row_ids[:, None] >= starts[None, :]) & (row_ids[:, None] < seg_ends[None, :])
    labels = jnp.arange(lengths.shape[0], dtype=jnp.int32)
    segment = lax.optimization_barrier(jnp.sum(jnp.where(inside, labels[None, :], 0), axis=1)).astype(jnp.int32)
    seg_begin = lax.optimization_barrier(jnp.sum(jnp.where(inside, starts[None, :], 0), axis=1)).astype(jnp.int32)
    return (segment, (row_ids - seg_begin).astype(jnp.int32))

def token_weight(advantage, ratio_log):
    keep_mask = jnp.where(advantage >= 0.0, ratio_log <= upper_log, ratio_log >= lower_log)
    return jnp.where(keep_mask, -advantage * jnp.exp(ratio_log), 0.0)

def rounded(tensor):
    return lax.optimization_barrier(tensor.astype(jnp.bfloat16)).astype(jnp.float32)

def attend_group(query_rows, grad_rows, query_index, query_segment, key_rows, value_heads, key_segment):
    row_count = query_rows.shape[0]
    groups = QH // KVH
    score_scale = 1.0 / math.sqrt(HD)
    query_f = query_rows.reshape(row_count, KVH, groups, HD).astype(jnp.float32)
    grad_f = grad_rows.reshape(row_count, KVH, groups, HD).astype(jnp.float32)
    keys_f = key_rows.astype(jnp.float32)
    values_f = value_heads.astype(jnp.float32)
    key_index = jnp.arange(key_rows.shape[0], dtype=jnp.int32)
    allowed = (query_segment[:, None] == key_segment[None, :]) & (key_index[None, :] <= query_index[:, None])
    scores = jnp.einsum('tkgd,jkd->kgtj', query_f, keys_f) * score_scale
    scores = jnp.where(allowed, scores, masked_score)
    row_peak = lax.optimization_barrier(jnp.max(scores, axis=-1, keepdims=True))
    exp_terms = jnp.where(allowed, jnp.exp(scores - row_peak), 0.0)
    soft_weights = exp_terms / lax.optimization_barrier(jnp.sum(exp_terms, axis=-1, keepdims=True))
    weights_b = soft_weights.astype(jnp.bfloat16).astype(jnp.float32)
    attn_out = jnp.einsum('kgtj,jkd->tkgd', weights_b, values_f)
    row_delta = jnp.einsum('tkgd,tkgd->kgt', grad_f, attn_out)
    prob_grad = jnp.einsum('tkgd,jkd->kgtj', grad_f, values_f)
    score_grad = (soft_weights * (prob_grad - row_delta[..., None])).astype(jnp.bfloat16).astype(jnp.float32)
    query_grad = (jnp.einsum('kgtj,jkd->tkgd', score_grad, keys_f) * score_scale).astype(jnp.bfloat16)
    key_part = jnp.einsum('kgtj,tkgd->jkd', score_grad, query_f) * score_scale
    value_part = jnp.einsum('kgtj,tkgd->jkd', weights_b, grad_f)
    return (query_grad.reshape(row_count, QH * HD), key_part, value_part)

def reference(hidden_in, norm_gain, key_weight, queries, logp_grad, values, advantages, log_ratio, resp_lengths, block_slots):
    row_ids = jnp.arange(STREAM, dtype=jnp.int32)
    gain_f = norm_gain.astype(jnp.float32)
    key_width = KVH * HD

    def one_stream(carry, stream_data):
        weight_acc, gain_acc = carry
        x_rows, query_rows, upstream, value_rows, advantage, ratio_log, lengths, slots = stream_data
        segment, position = segment_info(lengths, row_ids)
        x_float = x_rows.astype(jnp.float32)
        inv_rms = lax.rsqrt(lax.optimization_barrier(jnp.mean(x_float * x_float, axis=1, keepdims=True)) + norm_eps)
        normed = x_float * inv_rms
        normed_in = (normed * gain_f[None, :]).astype(jnp.bfloat16)
        raw_keys = jnp.dot(normed_in, key_weight, preferred_element_type=jnp.float32).reshape(STREAM, KVH, HD)
        cosine_table, sine_table = rope_tables(position, HD)
        key_rows = rotate(raw_keys, cosine_table, sine_table).astype(jnp.bfloat16)
        weight_tok = token_weight(advantage, ratio_log)
        out_grad = (weight_tok[:, None] * upstream.astype(jnp.float32)).astype(jnp.bfloat16)
        source_block = jnp.zeros((NBLK,), jnp.int32).at[slots].set(jnp.arange(NBLK, dtype=jnp.int32))
        order = (source_block[:, None] * BLK + jnp.arange(BLK, dtype=jnp.int32)[None, :]).reshape(STREAM)
        value_heads = value_rows.reshape(STREAM, KVH, HD)

        def one_group(sums, group_order):
            key_sum, value_sum = sums
            query_grad, key_part, value_part = attend_group(query_rows[group_order], out_grad[group_order], group_order, segment[group_order], key_rows, value_heads, segment)
            return ((key_sum + rounded(key_part), value_sum + rounded(value_part)), query_grad)
        empty = jnp.zeros((STREAM, KVH, HD), jnp.float32)
        (key_sum, value_sum), query_grads = lax.scan(one_group, (empty, empty), order.reshape(N_DP, TOK_DEV))
        value_grad = value_sum.astype(jnp.bfloat16).reshape(STREAM, key_width)
        raw_grad = rotate_back(key_sum, cosine_table, sine_table).astype(jnp.bfloat16).reshape(STREAM, key_width)
        normed_grad = jnp.dot(raw_grad, key_weight.T, preferred_element_type=jnp.float32).astype(jnp.bfloat16)
        weight_part = jnp.einsum('itd,itk->idk', normed_in.reshape(N_DP, TOK_DEV, D).astype(jnp.float32), raw_grad.reshape(N_DP, TOK_DEV, key_width).astype(jnp.float32))
        grad_f = normed_grad.astype(jnp.float32)
        gain_part = lax.optimization_barrier(jnp.sum((grad_f * normed).reshape(N_DP, TOK_DEV, D), axis=1))
        weight_acc = weight_acc + rounded(weight_part)
        gain_acc = gain_acc + rounded(gain_part)
        scaled = grad_f * gain_f[None, :]
        input_grad = (inv_rms * (scaled - normed * lax.optimization_barrier(jnp.mean(scaled * normed, axis=1, keepdims=True)))).astype(jnp.bfloat16)
        return ((weight_acc, gain_acc), (input_grad, query_grads.reshape(STREAM, QH * HD), value_grad))
    start_acc = (jnp.zeros((N_DP, D, key_width), jnp.float32), jnp.zeros((N_DP, D), jnp.float32))
    inputs_all = (hidden_in, queries, logp_grad, values, advantages, log_ratio, resp_lengths, block_slots)
    (weight_acc, gain_acc), (input_grad, query_grad, value_grad) = lax.scan(one_stream, start_acc, inputs_all)
    return (input_grad, query_grad, value_grad, weight_acc, gain_acc)
```

```python
import functools
import math

import jax
import jax.numpy as jnp
from jax import lax
from jax.experimental import pallas as pl
from jax.experimental.pallas import tpu as pltpu
from jax.sharding import PartitionSpec as P

HD = 128
QH = 32
KVH = 4
GROUPS = QH // KVH

norm_eps = 1e-05
rope_base = 500000.0
upper_log = math.log(1.2)
lower_log = math.log(0.8)
masked_score = -1e30
MESH = pl.DeviceIdType.MESH
F32 = jnp.float32
BF16 = jnp.bfloat16


def rope_tables(positions, head_size):
    half_size = head_size // 2
    frequency = rope_base ** (-(jnp.arange(half_size, dtype=F32) * 2.0) / head_size)
    angles = positions.astype(F32)[:, None] * frequency[None, :]
    return (jnp.cos(angles)[:, None, :], jnp.sin(angles)[:, None, :])


def rotate(tensor, cosine_table, sine_table):
    half_size = tensor.shape[-1] // 2
    a = tensor[..., :half_size]
    b = tensor[..., half_size:]
    return jnp.concatenate(
        [a * cosine_table - b * sine_table, b * cosine_table + a * sine_table], axis=-1
    )


def segment_starts(lengths, row_ids):
    seg_ends = jnp.cumsum(lengths)
    starts = seg_ends - lengths
    inside = (row_ids[:, None] >= starts[None, :]) & (row_ids[:, None] < seg_ends[None, :])
    return jnp.sum(jnp.where(inside, starts[None, :], 0), axis=1)


def token_weight(advantage, ratio_log):
    keep_mask = jnp.where(advantage >= 0.0, ratio_log <= upper_log, ratio_log >= lower_log)
    return jnp.where(keep_mask, -advantage * jnp.exp(ratio_log), 0.0)


def exchange_kernel(axis, n, modes, with_weight, n_shard, *refs):
    count = len(modes)
    ins = refs[: count + with_weight]
    outs = refs[count + with_weight : 2 * (count + with_weight)]
    rest = refs[2 * (count + with_weight) :]
    send_sem, recv_sem, local_sem = rest[:3]
    me = lax.axis_index(axis)
    barrier = pltpu.get_barrier_semaphore()
    for k in range(1, n):
        pl.semaphore_signal(
            barrier, inc=1, device_id={axis: lax.rem(me + k, n)}, device_id_type=MESH
        )
    greeted = n - 1
    if with_weight:
        z = lax.axis_index("shard")
        for k in range(1, n_shard):
            pl.semaphore_signal(
                barrier, inc=1, device_id={"shard": lax.rem(z + k, n_shard)}, device_id_type=MESH
            )
        greeted += n_shard - 1
    pl.semaphore_wait(barrier, greeted)

    w_copies = []
    if with_weight:
        wsend, wrecv, fsend, frecv, wloc = rest[3:]
        w_in, w_out = ins[count], outs[count]
        rows = w_in.shape[0]
        half_rows = rows // 2
        half = lax.rem(me, 2)
        mine = pl.ds(pl.multiple_of(half * half_rows, half_rows), half_rows)
        for k in range(1, n_shard):
            c = pltpu.make_async_remote_copy(
                src_ref=w_in.at[mine],
                dst_ref=w_out.at[z, mine],
                send_sem=wsend.at[k],
                recv_sem=wrecv.at[k],
                device_id={"shard": lax.rem(z + k, n_shard)},
                device_id_type=MESH,
            )
            c.start()
            w_copies.append(c)
    copies = []
    for a, mode in enumerate(modes):
        for k in range(1, n):
            peer = lax.rem(me + k, n)
            c = pltpu.make_async_remote_copy(
                src_ref=ins[a].at[peer] if mode == "a2a" else ins[a],
                dst_ref=outs[a].at[me],
                send_sem=send_sem.at[a, k],
                recv_sem=recv_sem.at[a, k],
                device_id={axis: peer},
                device_id_type=MESH,
            )
            c.start()
            copies.append(c)
    local_copies = []
    for a, mode in enumerate(modes):
        c = pltpu.make_async_copy(
            ins[a].at[me] if mode == "a2a" else ins[a], outs[a].at[me], local_sem.at[a]
        )
        c.start()
        local_copies.append(c)
    if with_weight:
        c = pltpu.make_async_copy(w_in, w_out.at[z], wloc)
        c.start()
        local_copies.append(c)
        sibling = me + 1 - 2 * half
        forwards = []
        for k in range(1, n_shard):
            src = lax.rem(z + n_shard - k, n_shard)
            pltpu.make_async_remote_copy(
                src_ref=w_in.at[mine],
                dst_ref=w_out.at[src, mine],
                send_sem=wsend.at[k],
                recv_sem=wrecv.at[k],
                device_id={"shard": lax.rem(z + k, n_shard)},
                device_id_type=MESH,
            ).wait_recv()
            c = pltpu.make_async_remote_copy(
                src_ref=w_out.at[src, mine],
                dst_ref=w_out.at[src, mine],
                send_sem=fsend.at[k],
                recv_sem=frecv.at[k],
                device_id={"dp": sibling},
                device_id_type=MESH,
            )
            c.start()
            forwards.append(c)
        other = pl.ds(pl.multiple_of((1 - half) * half_rows, half_rows), half_rows)
        for k in range(1, n_shard):
            src = lax.rem(z + n_shard - k, n_shard)
            pltpu.make_async_remote_copy(
                src_ref=w_out.at[src, other],
                dst_ref=w_out.at[src, other],
                send_sem=fsend.at[k],
                recv_sem=frecv.at[k],
                device_id={"dp": sibling},
                device_id_type=MESH,
            ).wait_recv()
        for c in forwards:
            c.wait_send()
        for c in w_copies:
            c.wait_send()
    for a, mode in enumerate(modes):
        for k in range(1, n):
            src = lax.rem(me + n - k, n)
            pltpu.make_async_remote_copy(
                src_ref=ins[a].at[src] if mode == "a2a" else ins[a],
                dst_ref=outs[a].at[src],
                send_sem=send_sem.at[a, k],
                recv_sem=recv_sem.at[a, k],
                device_id={axis: src},
                device_id_type=MESH,
            ).wait_recv()
    for c in copies:
        c.wait_send()
    for c in local_copies:
        c.wait()


def exchange(axis, arrays, modes, collective_id, weight=None):
    n = lax.axis_size(axis)
    n_shard = lax.axis_size("shard")
    outs = []
    for array, mode in zip(arrays, modes):
        block = array.shape[1:] if mode == "a2a" else array.shape
        outs.append(jax.ShapeDtypeStruct((n,) + block, array.dtype))
    sems = [
        pltpu.SemaphoreType.DMA((len(modes), n)),
        pltpu.SemaphoreType.DMA((len(modes), n)),
        pltpu.SemaphoreType.DMA((len(modes),)),
    ]
    operands = list(arrays)
    if weight is not None:
        operands.append(weight)
        outs.append(jax.ShapeDtypeStruct((n_shard,) + weight.shape, weight.dtype))
        sems += [pltpu.SemaphoreType.DMA((n_shard,))] * 4 + [pltpu.SemaphoreType.DMA]
    hbm = pl.BlockSpec(memory_space=pl.ANY)
    moved = sum(math.prod(o.shape) * o.dtype.itemsize for o in outs)
    return pl.pallas_call(
        functools.partial(
            exchange_kernel, axis, n, tuple(modes), int(weight is not None), n_shard
        ),
        out_shape=outs,
        in_specs=[hbm] * len(operands),
        out_specs=[hbm] * len(outs),
        scratch_shapes=sems,
        compiler_params=pltpu.CompilerParams(collective_id=collective_id, has_side_effects=True),
        cost_estimate=pl.CostEstimate(flops=0, bytes_accessed=20 * moved, transcendentals=0),
    )(*operands)


def pack_kernel(pick_ref, q_ref, g_ref, w_ref, out_ref):
    width = q_ref.shape[1]
    out_ref[0, :, :width] = q_ref[...]
    out_ref[0, :, width:] = (w_ref[...] * g_ref[...].astype(F32)).astype(BF16)


def pack_rows(pick, queries, logp, weight_col, block_rows, dp_size):
    width = queries.shape[1]
    return pl.pallas_call(
        pack_kernel,
        out_shape=jax.ShapeDtypeStruct((dp_size, block_rows, 2 * width), BF16),
        grid_spec=pltpu.PrefetchScalarGridSpec(
            num_scalar_prefetch=1,
            grid=(dp_size,),
            in_specs=[
                pl.BlockSpec((block_rows, width), lambda d, p: (p[d], 0)),
                pl.BlockSpec((block_rows, width), lambda d, p: (p[d], 0)),
                pl.BlockSpec((block_rows, 1), lambda d, p: (p[d], 0)),
            ],
            out_specs=pl.BlockSpec((1, block_rows, 2 * width), lambda d, p: (d, 0, 0)),
        ),
        cost_estimate=pl.CostEstimate(
            flops=0, bytes_accessed=8 * dp_size * block_rows * width, transcendentals=0
        ),
    )(pick, queries, logp, weight_col)


def dot_nt(a, b):
    return lax.dot_general(a, b, (((1,), (1,)), ((), ())), preferred_element_type=F32)


def dot_tn(a, b):
    return lax.dot_general(a, b, (((0,), (0,)), ((), ())), preferred_element_type=F32)


def attend_kernel(windows, src_ref, row_ref, low_ref, starts_ref, x_ref, k_ref, v_ref, qg_ref, kv_ref, dk, dv):
    slot = pl.program_id(0)
    stream_len = dk.shape[0]
    block_rows = x_ref.shape[1]
    half = QH * HD
    scale = 1.0 / math.sqrt(HD)
    first_row = row_ref[slot]
    low = (low_ref[slot] // 128) * 128
    span = first_row + block_rows - low

    @pl.when(slot == 0)
    def _():
        dk[...] = jnp.zeros_like(dk)
        dv[...] = jnp.zeros_like(dv)

    m_rows = GROUPS * block_rows
    pos = first_row + lax.rem(lax.broadcasted_iota(jnp.int32, (m_rows, 1), 0), block_rows)
    seg_low = jnp.zeros_like(pos)
    for r in range(1, starts_ref.shape[0]):
        seg_low = jnp.where(pos >= starts_ref[r], starts_ref[r], seg_low)

    def body(width):
        start = pl.multiple_of(jnp.minimum(low, stream_len - width), 128)
        j = start + lax.broadcasted_iota(jnp.int32, (m_rows, width), 1)
        allowed = (j >= seg_low) & (j <= pos)
        rows = pl.ds(start, width)
        for h in range(KVH):
            cols = slice(h * HD, (h + 1) * HD)
            base = h * GROUPS * HD
            q = jnp.concatenate(
                [x_ref[0, :, base + g * HD : base + (g + 1) * HD] for g in range(GROUPS)], axis=0
            )
            og = jnp.concatenate(
                [
                    x_ref[0, :, half + base + g * HD : half + base + (g + 1) * HD]
                    for g in range(GROUPS)
                ],
                axis=0,
            )
            k = k_ref[rows, cols]
            v = v_ref[rows, cols]
            s = jnp.where(allowed, dot_nt(q, k) * scale, masked_score)
            e = jnp.exp(s - jnp.max(s, axis=1, keepdims=True))
            p = e * (1.0 / jnp.sum(e, axis=1, keepdims=True))
            pb = p.astype(BF16)
            dp = dot_nt(og, v)
            delta = jnp.sum(pb.astype(F32) * dp, axis=1, keepdims=True)
            ds = (p * (dp - delta)).astype(BF16)
            dq = (jnp.dot(ds, k, preferred_element_type=F32) * scale).astype(BF16)
            for g in range(GROUPS):
                qg_ref[:, base + g * HD : base + (g + 1) * HD] = dq[
                    g * block_rows : (g + 1) * block_rows
                ]
            dk[rows, cols] += dot_tn(ds, q)
            dv[rows, cols] += dot_tn(pb, og)

    before = 0
    for width in windows:
        last = width == windows[-1]
        fits = (span > before) if last else (span > before) & (span <= width)

        @pl.when(fits)
        def _(width=width):
            body(width)

        before = width

    @pl.when(slot == pl.num_programs(0) - 1)
    def _():
        kw = dk.shape[1]
        kv_ref[:, :kw] = (dk[...] * scale).astype(BF16)
        kv_ref[:, kw:] = dv[...].astype(BF16)


def attend(src, first_row, low, starts, incoming, keys, values):
    stream_len, kw = keys.shape
    slots = src.shape[0]
    block_rows = incoming.shape[1]
    windows = tuple(w for w in (128, 256, 384, 512, 640, 768) if w < stream_len) + (stream_len,)
    whole = lambda s, *_: (0, 0)
    return pl.pallas_call(
        functools.partial(attend_kernel, windows),
        out_shape=[
            jax.ShapeDtypeStruct((slots * block_rows, QH * HD), BF16),
            jax.ShapeDtypeStruct((stream_len, 2 * kw), BF16),
        ],
        grid_spec=pltpu.PrefetchScalarGridSpec(
            num_scalar_prefetch=4,
            grid=(slots,),
            in_specs=[
                pl.BlockSpec((1, block_rows, incoming.shape[2]), lambda s, a, *_: (a[s], 0, 0)),
                pl.BlockSpec((stream_len, kw), whole),
                pl.BlockSpec((stream_len, kw), whole),
            ],
            out_specs=[
                pl.BlockSpec((block_rows, QH * HD), lambda s, *_: (s, 0)),
                pl.BlockSpec((stream_len, 2 * kw), whole),
            ],
            scratch_shapes=[pltpu.VMEM((stream_len, kw), F32), pltpu.VMEM((stream_len, kw), F32)],
        ),
        compiler_params=pltpu.CompilerParams(vmem_limit_bytes=48 * 1024 * 1024),
        cost_estimate=pl.CostEstimate(
            flops=20_000_000_000, bytes_accessed=60_000_000, transcendentals=4_000_000
        ),
    )(src, first_row, low, starts, incoming, keys, values)


def local(
    hidden_in,
    norm_gain,
    key_weight,
    queries,
    logp_grad,
    values,
    advantages,
    log_ratio,
    resp_lengths,
    block_slots,
):
    row_count, width = hidden_in.shape[1:]
    dp_size = lax.axis_size("dp")
    n_shard = lax.axis_size("shard")
    stream_len = row_count * dp_size
    blocks_dev = block_slots.shape[1]
    block_rows = row_count // blocks_dev
    slice_w, key_width = key_weight.shape
    here = lax.axis_index("dp")
    z = lax.axis_index("shard")
    row_ids = here * row_count + jnp.arange(row_count, dtype=jnp.int32)
    lengths = resp_lengths[0]
    starts = jnp.cumsum(lengths) - lengths
    position = row_ids - segment_starts(lengths, row_ids)

    slot_list = block_slots[0]
    dest_dev = slot_list // blocks_dev
    block_ids = jnp.arange(blocks_dev, dtype=jnp.int32)
    dev_ids = jnp.arange(dp_size, dtype=jnp.int32)
    pick = jnp.sum(jnp.where(dest_dev[None, :] == dev_ids[:, None], block_ids[None, :], 0), axis=1)
    weight_tok = token_weight(advantages[0], log_ratio[0])
    outgoing = pack_rows(
        pick, queries[0], logp_grad[0], weight_tok[:, None], block_rows, dp_size
    )
    slot_tile = jnp.broadcast_to(slot_list[:, None], (blocks_dev, 128))
    incoming, table, all_values, full_weight = exchange(
        "dp", [outgoing, slot_tile, values[0]], ["a2a", "ag", "ag"], 1, weight=key_weight
    )
    full_weight = full_weight.reshape(width, key_width)

    pieces = []
    for k in range(n_shard):
        target = lax.rem(z + k, n_shard)
        piece = lax.dynamic_slice_in_dim(hidden_in[0], target * slice_w, slice_w, 1)
        if k:
            piece = lax.ppermute(piece, "shard", [(i, (i + k) % n_shard) for i in range(n_shard)])
        pieces.append(piece)

    x_float = hidden_in[0].astype(F32)
    inv_rms = lax.rsqrt(jnp.mean(x_float * x_float, axis=1, keepdims=True) + norm_eps)
    normed = x_float * inv_rms
    gain_f = norm_gain.astype(F32)
    normed_in = (normed * gain_f[None, :]).astype(BF16)
    raw_keys = jnp.dot(normed_in, full_weight, preferred_element_type=F32)
    cosine_table, sine_table = rope_tables(position, HD)
    key_rows = (
        rotate(raw_keys.reshape(row_count, KVH, HD), cosine_table, sine_table)
        .astype(BF16)
        .reshape(row_count, key_width)
    )
    (all_keys,) = exchange("dp", [key_rows], ["ag"], 2)

    slot_table = table[:, :, 0].reshape(-1)
    my_slots = here * blocks_dev + block_ids
    all_blocks = jnp.arange(slot_table.shape[0], dtype=jnp.int32)
    source_block = jnp.sum(
        jnp.where(slot_table[None, :] == my_slots[:, None], all_blocks[None, :], 0), axis=1
    )
    first_row = source_block * block_rows
    low = segment_starts(lengths, first_row)
    query_grad, kv_part = attend(
        source_block // blocks_dev,
        first_row,
        low,
        starts,
        incoming,
        all_keys.reshape(stream_len, key_width),
        all_values.reshape(stream_len, key_width),
    )
    (parts,) = exchange("dp", [kv_part.reshape(dp_size, row_count, 2 * key_width)], ["a2a"], 3)
    kv_sum = jnp.sum(parts.astype(F32), axis=0)
    value_grad = kv_sum[:, key_width:].astype(BF16)
    raw_grad = (
        rotate(kv_sum[:, :key_width].reshape(row_count, KVH, HD), cosine_table, -sine_table)
        .astype(BF16)
        .reshape(row_count, key_width)
    )
    inv_tile = jnp.broadcast_to(inv_rms, (row_count, 128))
    raw_all, inv_all = exchange("shard", [raw_grad, inv_tile], ["ag", "ag"], 4)

    normed_grad = dot_nt(raw_grad, full_weight).astype(BF16)
    grad_f = normed_grad.astype(F32)
    scaled = grad_f * gain_f[None, :]
    input_grad = (
        inv_rms * (scaled - normed * jnp.mean(scaled * normed, axis=1, keepdims=True))
    ).astype(BF16)

    gain_own = lax.dynamic_slice_in_dim(gain_f, z * slice_w, slice_w, 0)
    weight_grad = jnp.zeros((slice_w, key_width), F32)
    gain_grad = jnp.zeros((slice_w,), F32)
    for k in range(n_shard):
        source = lax.rem(z + n_shard - k, n_shard)
        raw_k = lax.dynamic_index_in_dim(raw_all, source, 0, keepdims=False)
        inv_k = lax.dynamic_index_in_dim(inv_all, source, 0, keepdims=False)[:, :1]
        normed_k = pieces[k].astype(F32) * inv_k
        in_k = (normed_k * gain_own[None, :]).astype(BF16)
        weight_grad += dot_tn(in_k, raw_k).astype(BF16).astype(F32)
        grad_k = dot_nt(raw_k, key_weight).astype(BF16).astype(F32)
        gain_grad += jnp.sum(grad_k * normed_k, axis=0).astype(BF16).astype(F32)
    return (
        input_grad[None],
        query_grad[None],
        value_grad[None],
        weight_grad[None],
        gain_grad[None],
    )


def solution(mesh):
    placed = (
        P("shard", "dp", None),
        P(),
        P("shard", None),
        P("shard", "dp", None),
        P("shard", "dp", None),
        P("shard", "dp", None),
        P("shard", "dp"),
        P("shard", "dp"),
        P("shard", None),
        P("shard", "dp"),
    )
    return jax.shard_map(
        local,
        mesh=mesh,
        in_specs=placed,
        out_specs=(
            P("shard", "dp", None),
            P("shard", "dp", None),
            P("shard", "dp", None),
            P("dp", "shard", None),
            P("dp", "shard"),
        ),
        check_vma=False,
    )
```

```python
import functools
import math

import jax
import jax.numpy as jnp
from jax import lax
from jax.experimental import pallas as pl
from jax.experimental.pallas import tpu as pltpu
from jax.sharding import PartitionSpec as P

HD = 128
QH = 32
KVH = 4
GROUPS = QH // KVH

norm_eps = 1e-05
rope_base = 500000.0
upper_log = math.log(1.2)
lower_log = math.log(0.8)
masked_score = -1e30
MESH = pl.DeviceIdType.MESH
F32 = jnp.float32
BF16 = jnp.bfloat16


def rope_tables(positions, head_size):
    half_size = head_size // 2
    frequency = rope_base ** (-(jnp.arange(half_size, dtype=F32) * 2.0) / head_size)
    angles = positions.astype(F32)[:, None] * frequency[None, :]
    return (jnp.cos(angles)[:, None, :], jnp.sin(angles)[:, None, :])


def segment_starts(lengths, row_ids):
    seg_ends = jnp.cumsum(lengths)
    starts = seg_ends - lengths
    inside = (row_ids[:, None] >= starts[None, :]) & (row_ids[:, None] < seg_ends[None, :])
    return jnp.sum(jnp.where(inside, starts[None, :], 0), axis=1)


def token_weight(advantage, ratio_log):
    keep_mask = jnp.where(advantage >= 0.0, ratio_log <= upper_log, ratio_log >= lower_log)
    return jnp.where(keep_mask, -advantage * jnp.exp(ratio_log), 0.0)


def exchange_kernel(axis, n, modes, with_weight, n_shard, *refs):
    count = len(modes)
    ins = refs[: count + with_weight]
    outs = refs[count + with_weight : 2 * (count + with_weight)]
    rest = refs[2 * (count + with_weight) :]
    send_sem, recv_sem, local_sem = rest[:3]
    me = lax.axis_index(axis)
    barrier = pltpu.get_barrier_semaphore()
    for k in range(1, n):
        pl.semaphore_signal(
            barrier, inc=1, device_id={axis: lax.rem(me + k, n)}, device_id_type=MESH
        )
    greeted = n - 1
    if with_weight:
        z = lax.axis_index("shard")
        for k in range(1, n_shard):
            pl.semaphore_signal(
                barrier, inc=1, device_id={"shard": lax.rem(z + k, n_shard)}, device_id_type=MESH
            )
        greeted += n_shard - 1
    pl.semaphore_wait(barrier, greeted)

    w_copies = []
    if with_weight:
        wsend, wrecv, fsend, frecv, nsend, nrecv, gsend, grecv, wloc = rest[3:]
        w_in, w_out = ins[count], outs[count]
        part_rows = w_in.shape[0] // 4
        core = lax.rem(me, 2)
        bit1 = lax.rem(lax.div(me, 2), 2)
        bit2 = lax.rem(lax.div(me, 4), 2)
        color = lax.rem(bit1 + bit2, 2)
        sibling = me + 1 - 2 * core
        neighbour = me + (1 - core) * (2 - 4 * bit1) + core * (4 - 8 * bit2)

        def part(index):
            return pl.ds(pl.multiple_of(index * part_rows, part_rows), part_rows)

        mine = part(2 * color + core)
        theirs = part(2 * (1 - color) + core)
        sib_mine = part(2 * color + 1 - core)
        sib_theirs = part(2 * (1 - color) + 1 - core)

        def over_z(k):
            return pltpu.make_async_remote_copy(
                src_ref=w_in.at[mine],
                dst_ref=w_out.at[z, mine],
                send_sem=wsend.at[k],
                recv_sem=wrecv.at[k],
                device_id={"shard": lax.rem(z + k, n_shard)},
                device_id_type=MESH,
            )

        def hand_on(source, rows, send, recv, k, target):
            return pltpu.make_async_remote_copy(
                src_ref=w_out.at[source, rows],
                dst_ref=w_out.at[source, rows],
                send_sem=send.at[k],
                recv_sem=recv.at[k],
                device_id={"dp": target},
                device_id_type=MESH,
            )

        for k in range(1, n_shard):
            c = over_z(k)
            c.start()
            w_copies.append(c)
    copies = []
    for a, mode in enumerate(modes):
        for k in range(1, n):
            peer = lax.rem(me + k, n)
            c = pltpu.make_async_remote_copy(
                src_ref=ins[a].at[peer] if mode == "a2a" else ins[a],
                dst_ref=outs[a].at[me],
                send_sem=send_sem.at[a, k],
                recv_sem=recv_sem.at[a, k],
                device_id={axis: peer},
                device_id_type=MESH,
            )
            c.start()
            copies.append(c)
    local_copies = []
    for a, mode in enumerate(modes):
        c = pltpu.make_async_copy(
            ins[a].at[me] if mode == "a2a" else ins[a], outs[a].at[me], local_sem.at[a]
        )
        c.start()
        local_copies.append(c)
    if with_weight:
        c = pltpu.make_async_copy(w_in, w_out.at[z], wloc)
        c.start()
        local_copies.append(c)
        sources = [lax.rem(z + n_shard - k, n_shard) for k in range(n_shard)]
        for k in range(1, n_shard):
            pltpu.make_async_remote_copy(
                src_ref=w_in.at[mine],
                dst_ref=w_out.at[sources[k], mine],
                send_sem=wsend.at[k],
                recv_sem=wrecv.at[k],
                device_id={"shard": lax.rem(z + k, n_shard)},
                device_id_type=MESH,
            ).wait_recv()
            for c in (
                hand_on(sources[k], mine, nsend, nrecv, k, neighbour),
                hand_on(sources[k], mine, fsend, frecv, k, sibling),
            ):
                c.start()
                w_copies.append(c)
        for k in range(1, n_shard):
            hand_on(sources[k], theirs, nsend, nrecv, k, neighbour).wait_recv()
            c = hand_on(sources[k], theirs, gsend, grecv, k, sibling)
            c.start()
            w_copies.append(c)
        for k in range(1, n_shard):
            hand_on(sources[k], sib_mine, fsend, frecv, k, sibling).wait_recv()
            hand_on(sources[k], sib_theirs, gsend, grecv, k, sibling).wait_recv()
        for c in w_copies:
            c.wait_send()
    for a, mode in enumerate(modes):
        for k in range(1, n):
            src = lax.rem(me + n - k, n)
            pltpu.make_async_remote_copy(
                src_ref=ins[a].at[src] if mode == "a2a" else ins[a],
                dst_ref=outs[a].at[src],
                send_sem=send_sem.at[a, k],
                recv_sem=recv_sem.at[a, k],
                device_id={axis: src},
                device_id_type=MESH,
            ).wait_recv()
    for c in copies:
        c.wait_send()
    for c in local_copies:
        c.wait()


def exchange(axis, arrays, modes, collective_id, weight=None):
    n = lax.axis_size(axis)
    n_shard = lax.axis_size("shard")
    outs = []
    for array, mode in zip(arrays, modes):
        block = array.shape[1:] if mode == "a2a" else array.shape
        outs.append(jax.ShapeDtypeStruct((n,) + block, array.dtype))
    sems = [
        pltpu.SemaphoreType.DMA((len(modes), n)),
        pltpu.SemaphoreType.DMA((len(modes), n)),
        pltpu.SemaphoreType.DMA((len(modes),)),
    ]
    operands = list(arrays)
    if weight is not None:
        operands.append(weight)
        outs.append(jax.ShapeDtypeStruct((n_shard,) + weight.shape, weight.dtype))
        sems += [pltpu.SemaphoreType.DMA((n_shard,))] * 8 + [pltpu.SemaphoreType.DMA]
    hbm = pl.BlockSpec(memory_space=pl.ANY)
    moved = sum(math.prod(o.shape) * o.dtype.itemsize for o in outs)
    return pl.pallas_call(
        functools.partial(
            exchange_kernel, axis, n, tuple(modes), int(weight is not None), n_shard
        ),
        out_shape=outs,
        in_specs=[hbm] * len(operands),
        out_specs=[hbm] * len(outs),
        scratch_shapes=sems,
        compiler_params=pltpu.CompilerParams(collective_id=collective_id, has_side_effects=True),
        cost_estimate=pl.CostEstimate(flops=0, bytes_accessed=20 * moved, transcendentals=0),
    )(*operands)


def pack_kernel(pick_ref, q_ref, g_ref, w_ref, out_ref):
    width = q_ref.shape[1]
    out_ref[0, :, :width] = q_ref[...]
    out_ref[0, :, width:] = (w_ref[...] * g_ref[...].astype(F32)).astype(BF16)


def pack_rows(pick, queries, logp, weight_col, block_rows, dp_size):
    width = queries.shape[1]
    return pl.pallas_call(
        pack_kernel,
        out_shape=jax.ShapeDtypeStruct((dp_size, block_rows, 2 * width), BF16),
        grid_spec=pltpu.PrefetchScalarGridSpec(
            num_scalar_prefetch=1,
            grid=(dp_size,),
            in_specs=[
                pl.BlockSpec((block_rows, width), lambda d, p: (p[d], 0)),
                pl.BlockSpec((block_rows, width), lambda d, p: (p[d], 0)),
                pl.BlockSpec((block_rows, 1), lambda d, p: (p[d], 0)),
            ],
            out_specs=pl.BlockSpec((1, block_rows, 2 * width), lambda d, p: (d, 0, 0)),
        ),
        cost_estimate=pl.CostEstimate(
            flops=0, bytes_accessed=8 * dp_size * block_rows * width, transcendentals=0
        ),
    )(pick, queries, logp, weight_col)


def dot_nt(a, b):
    return lax.dot_general(a, b, (((1,), (1,)), ((), ())), preferred_element_type=F32)


def dot_tn(a, b):
    return lax.dot_general(a, b, (((0,), (0,)), ((), ())), preferred_element_type=F32)


def attend_kernel(windows, src_ref, row_ref, low_ref, starts_ref, x_ref, k_ref, v_ref, qg_ref, kv_ref, dk, dv):
    slot = pl.program_id(0)
    stream_len = dk.shape[0]
    block_rows = x_ref.shape[1]
    half = QH * HD
    scale = 1.0 / math.sqrt(HD)
    first_row = row_ref[slot]
    low = (low_ref[slot] // 128) * 128
    span = first_row + block_rows - low

    @pl.when(slot == 0)
    def _():
        dk[...] = jnp.zeros_like(dk)
        dv[...] = jnp.zeros_like(dv)

    m_rows = GROUPS * block_rows
    pos = first_row + lax.rem(lax.broadcasted_iota(jnp.int32, (m_rows, 1), 0), block_rows)
    seg_low = jnp.zeros_like(pos)
    for r in range(1, starts_ref.shape[0]):
        seg_low = jnp.where(pos >= starts_ref[r], starts_ref[r], seg_low)

    def body(width):
        start = pl.multiple_of(jnp.minimum(low, stream_len - width), 128)
        j = start + lax.broadcasted_iota(jnp.int32, (m_rows, width), 1)
        allowed = (j >= seg_low) & (j <= pos)
        rows = pl.ds(start, width)
        for h in range(KVH):
            cols = slice(h * HD, (h + 1) * HD)
            base = h * GROUPS * HD
            q = jnp.concatenate(
                [x_ref[0, :, base + g * HD : base + (g + 1) * HD] for g in range(GROUPS)], axis=0
            )
            og = jnp.concatenate(
                [
                    x_ref[0, :, half + base + g * HD : half + base + (g + 1) * HD]
                    for g in range(GROUPS)
                ],
                axis=0,
            )
            k = k_ref[rows, cols]
            v = v_ref[rows, cols]
            s = jnp.where(allowed, dot_nt(q, k) * scale, masked_score)
            e = jnp.exp(s - jnp.max(s, axis=1, keepdims=True))
            p = e * (1.0 / jnp.sum(e, axis=1, keepdims=True))
            pb = p.astype(BF16)
            dp = dot_nt(og, v)
            delta = jnp.sum(pb.astype(F32) * dp, axis=1, keepdims=True)
            ds = (p * (dp - delta)).astype(BF16)
            dq = (jnp.dot(ds, k, preferred_element_type=F32) * scale).astype(BF16)
            for g in range(GROUPS):
                qg_ref[:, base + g * HD : base + (g + 1) * HD] = dq[
                    g * block_rows : (g + 1) * block_rows
                ]
            dk[rows, cols] += dot_tn(ds, q)
            dv[rows, cols] += dot_tn(pb, og)

    before = 0
    for width in windows:
        last = width == windows[-1]
        fits = (span > before) if last else (span > before) & (span <= width)

        @pl.when(fits)
        def _(width=width):
            body(width)

        before = width

    @pl.when(slot == pl.num_programs(0) - 1)
    def _():
        kw = dk.shape[1]
        kv_ref[:, :kw] = (dk[...] * scale).astype(BF16)
        kv_ref[:, kw:] = dv[...].astype(BF16)


def attend(src, first_row, low, starts, incoming, keys, values):
    stream_len, kw = keys.shape
    slots = src.shape[0]
    block_rows = incoming.shape[1]
    windows = tuple(w for w in (128, 256, 384, 512, 640, 768) if w < stream_len) + (stream_len,)
    whole = lambda s, *_: (0, 0)
    return pl.pallas_call(
        functools.partial(attend_kernel, windows),
        out_shape=[
            jax.ShapeDtypeStruct((slots * block_rows, QH * HD), BF16),
            jax.ShapeDtypeStruct((stream_len, 2 * kw), BF16),
        ],
        grid_spec=pltpu.PrefetchScalarGridSpec(
            num_scalar_prefetch=4,
            grid=(slots,),
            in_specs=[
                pl.BlockSpec((1, block_rows, incoming.shape[2]), lambda s, a, *_: (a[s], 0, 0)),
                pl.BlockSpec((stream_len, kw), whole),
                pl.BlockSpec((stream_len, kw), whole),
            ],
            out_specs=[
                pl.BlockSpec((block_rows, QH * HD), lambda s, *_: (s, 0)),
                pl.BlockSpec((stream_len, 2 * kw), whole),
            ],
            scratch_shapes=[pltpu.VMEM((stream_len, kw), F32), pltpu.VMEM((stream_len, kw), F32)],
        ),
        compiler_params=pltpu.CompilerParams(vmem_limit_bytes=48 * 1024 * 1024),
        cost_estimate=pl.CostEstimate(
            flops=20_000_000_000, bytes_accessed=60_000_000, transcendentals=4_000_000
        ),
    )(src, first_row, low, starts, incoming, keys, values)


def keys_kernel(x_ref, w_ref, gain_ref, cos_ref, sin_ref, key_ref, inv_ref, acc, inv):
    step = pl.program_id(0)
    chunk = w_ref.shape[0]
    width = x_ref.shape[1]

    @pl.when(step == 0)
    def _():
        total = jnp.zeros((x_ref.shape[0], 1), F32)
        for c in range(0, width, 1024):
            x = x_ref[:, c : c + 1024].astype(F32)
            total += jnp.sum(x * x, axis=1, keepdims=True)
        inv[...] = lax.rsqrt(total / width + norm_eps)
        inv_ref[...] = jnp.broadcast_to(inv[...], inv_ref.shape)
        acc[...] = jnp.zeros_like(acc)

    cols = pl.ds(pl.multiple_of(step * chunk, chunk), chunk)
    normed = x_ref[:, cols].astype(F32) * inv[...]
    normed_in = (normed * gain_ref[:, cols].astype(F32)).astype(BF16)
    acc[...] += jnp.dot(normed_in, w_ref[...], preferred_element_type=F32)

    @pl.when(step == pl.num_programs(0) - 1)
    def _():
        half = HD // 2
        cos, sin = cos_ref[...], sin_ref[...]
        for h in range(KVH):
            a = acc[:, h * HD : h * HD + half]
            b = acc[:, h * HD + half : (h + 1) * HD]
            key_ref[:, h * HD : (h + 1) * HD] = jnp.concatenate(
                [a * cos - b * sin, b * cos + a * sin], axis=1
            ).astype(BF16)


def make_keys(x, weight, gain, cos, sin):
    rows, width = x.shape
    kw = weight.shape[1]
    chunk = 1024
    whole = lambda c: (0, 0)
    return pl.pallas_call(
        keys_kernel,
        out_shape=[
            jax.ShapeDtypeStruct((rows, kw), BF16),
            jax.ShapeDtypeStruct((rows, 128), F32),
        ],
        grid=(width // chunk,),
        in_specs=[
            pl.BlockSpec((rows, width), whole),
            pl.BlockSpec((chunk, kw), lambda c: (c, 0)),
            pl.BlockSpec((1, width), whole),
            pl.BlockSpec(cos.shape, whole),
            pl.BlockSpec(sin.shape, whole),
        ],
        out_specs=[pl.BlockSpec((rows, kw), whole), pl.BlockSpec((rows, 128), whole)],
        scratch_shapes=[pltpu.VMEM((rows, kw), F32), pltpu.VMEM((rows, 1), F32)],
        compiler_params=pltpu.CompilerParams(vmem_limit_bytes=40 * 1024 * 1024),
        cost_estimate=pl.CostEstimate(
            flops=2 * rows * width * kw, bytes_accessed=4 * width * kw, transcendentals=0
        ),
    )(x, weight, gain, cos, sin)


def raw_kernel(parts_ref, cos_ref, sin_ref, raw_ref, value_ref):
    kw = raw_ref.shape[1]
    half = HD // 2
    total = parts_ref[0].astype(F32)
    for i in range(1, parts_ref.shape[0]):
        total += parts_ref[i].astype(F32)
    value_ref[...] = total[:, kw:].astype(BF16)
    cos, sin = cos_ref[...], sin_ref[...]
    for h in range(KVH):
        a = total[:, h * HD : h * HD + half]
        b = total[:, h * HD + half : (h + 1) * HD]
        raw_ref[:, h * HD : (h + 1) * HD] = jnp.concatenate(
            [a * cos + b * sin, b * cos - a * sin], axis=1
        ).astype(BF16)


def make_raw(parts, cos, sin):
    rows = parts.shape[1]
    kw = parts.shape[2] // 2
    return pl.pallas_call(
        raw_kernel,
        out_shape=[jax.ShapeDtypeStruct((rows, kw), BF16)] * 2,
        compiler_params=pltpu.CompilerParams(vmem_limit_bytes=40 * 1024 * 1024),
    )(parts, cos, sin)


def rows_kernel(raw_ref, w_ref, x_ref, inv_ref, gain_ref, out_ref, grads, total):
    step = pl.program_id(0)
    chunk = w_ref.shape[0]
    width = x_ref.shape[1]
    inv = inv_ref[:, :1]

    @pl.when(step == 0)
    def _():
        total[...] = jnp.zeros_like(total)

    cols = pl.ds(pl.multiple_of(step * chunk, chunk), chunk)
    grad = dot_nt(raw_ref[...], w_ref[...]).astype(BF16)
    grads[:, cols] = grad
    scaled = grad.astype(F32) * gain_ref[:, cols].astype(F32)
    normed = x_ref[:, cols].astype(F32) * inv
    total[...] += jnp.sum(scaled * normed, axis=1, keepdims=True)

    @pl.when(step == pl.num_programs(0) - 1)
    def _():
        mean = total[...] / width
        for c in range(0, width, 1024):
            part = slice(c, c + 1024)
            scaled = grads[:, part].astype(F32) * gain_ref[:, part].astype(F32)
            normed = x_ref[:, part].astype(F32) * inv
            out_ref[:, part] = (inv * (scaled - normed * mean)).astype(BF16)


def own_rows(raw, weight, x, inv, gain):
    rows, width = x.shape
    kw = weight.shape[1]
    chunk = 1024
    whole = lambda c: (0, 0)
    return pl.pallas_call(
        rows_kernel,
        out_shape=jax.ShapeDtypeStruct((rows, width), BF16),
        grid=(width // chunk,),
        in_specs=[
            pl.BlockSpec((rows, kw), whole),
            pl.BlockSpec((chunk, kw), lambda c: (c, 0)),
            pl.BlockSpec((rows, width), whole),
            pl.BlockSpec((rows, 128), whole),
            pl.BlockSpec((1, width), whole),
        ],
        out_specs=pl.BlockSpec((rows, width), whole),
        scratch_shapes=[pltpu.VMEM((rows, width), BF16), pltpu.VMEM((rows, 1), F32)],
        compiler_params=pltpu.CompilerParams(vmem_limit_bytes=40 * 1024 * 1024),
        cost_estimate=pl.CostEstimate(
            flops=2 * rows * width * kw, bytes_accessed=4 * width * kw, transcendentals=0
        ),
    )(raw, weight, x, inv, gain)


def own_kernel(n, z_ref, raw_ref, inv_ref, w_ref, gain_ref, *refs):
    pieces, (wg_ref, gg_ref) = refs[:n], refs[n:]
    z = z_ref[0]
    gain = gain_ref[...].astype(F32)
    weight = w_ref[...]
    weight_sum = None
    for k in range(n):
        source = lax.rem(z + n - k, n)
        raw = raw_ref[source]
        inv = inv_ref[source][:, :1]
        normed = pieces[k][...].astype(F32) * inv
        term = dot_tn((normed * gain).astype(BF16), raw).astype(BF16).astype(F32)
        grad = dot_nt(raw, weight).astype(BF16).astype(F32)
        row = jnp.sum(grad * normed, axis=0, keepdims=True).astype(BF16).astype(F32)
        weight_sum = term if k == 0 else weight_sum + term
        gain_sum = row if k == 0 else gain_sum + row
    wg_ref[...] = weight_sum
    gg_ref[...] = gain_sum


def own_weight(z, raw_all, inv_all, weight, gain, pieces):
    n, rows, kw = raw_all.shape
    slice_w = weight.shape[0]
    chunk = min(256, slice_w)
    steps = slice_w // chunk
    whole = lambda c, zr: (0, 0, 0)
    return pl.pallas_call(
        functools.partial(own_kernel, n),
        out_shape=[
            jax.ShapeDtypeStruct((slice_w, kw), F32),
            jax.ShapeDtypeStruct((1, slice_w), F32),
        ],
        grid_spec=pltpu.PrefetchScalarGridSpec(
            num_scalar_prefetch=1,
            grid=(steps,),
            in_specs=[
                pl.BlockSpec(raw_all.shape, whole),
                pl.BlockSpec(inv_all.shape, whole),
                pl.BlockSpec((chunk, kw), lambda c, zr: (c, 0)),
                pl.BlockSpec((1, chunk), lambda c, zr: (0, zr[0] * steps + c)),
            ]
            + [pl.BlockSpec((rows, chunk), lambda c, zr: (0, c))] * n,
            out_specs=[
                pl.BlockSpec((chunk, kw), lambda c, zr: (c, 0)),
                pl.BlockSpec((1, chunk), lambda c, zr: (0, c)),
            ],
        ),
        compiler_params=pltpu.CompilerParams(vmem_limit_bytes=40 * 1024 * 1024),
        cost_estimate=pl.CostEstimate(
            flops=4 * n * rows * slice_w * kw, bytes_accessed=12 * slice_w * kw, transcendentals=0
        ),
    )(z.reshape(1), raw_all, inv_all, weight, gain, *pieces)


def local(
    hidden_in,
    norm_gain,
    key_weight,
    queries,
    logp_grad,
    values,
    advantages,
    log_ratio,
    resp_lengths,
    block_slots,
):
    row_count, width = hidden_in.shape[1:]
    dp_size = lax.axis_size("dp")
    n_shard = lax.axis_size("shard")
    stream_len = row_count * dp_size
    blocks_dev = block_slots.shape[1]
    block_rows = row_count // blocks_dev
    slice_w, key_width = key_weight.shape
    here = lax.axis_index("dp")
    z = lax.axis_index("shard")
    row_ids = here * row_count + jnp.arange(row_count, dtype=jnp.int32)
    lengths = resp_lengths[0]
    starts = jnp.cumsum(lengths) - lengths
    position = row_ids - segment_starts(lengths, row_ids)

    slot_list = block_slots[0]
    dest_dev = slot_list // blocks_dev
    block_ids = jnp.arange(blocks_dev, dtype=jnp.int32)
    dev_ids = jnp.arange(dp_size, dtype=jnp.int32)
    pick = jnp.sum(jnp.where(dest_dev[None, :] == dev_ids[:, None], block_ids[None, :], 0), axis=1)
    weight_tok = token_weight(advantages[0], log_ratio[0])
    outgoing = pack_rows(
        pick, queries[0], logp_grad[0], weight_tok[:, None], block_rows, dp_size
    )
    slot_tile = jnp.broadcast_to(slot_list[:, None], (blocks_dev, 128))
    incoming, table, all_values, full_weight = exchange(
        "dp", [outgoing, slot_tile, values[0]], ["a2a", "ag", "ag"], 1, weight=key_weight
    )
    full_weight = full_weight.reshape(width, key_width)

    pieces = []
    for k in range(n_shard):
        target = lax.rem(z + k, n_shard)
        pieces.append(lax.dynamic_slice_in_dim(hidden_in[0], target * slice_w, slice_w, 1))
    pieces, full_weight = lax.optimization_barrier((pieces, full_weight))
    for k in range(1, n_shard):
        pieces[k] = lax.ppermute(
            pieces[k], "shard", [(i, (i + k) % n_shard) for i in range(n_shard)]
        )

    gain_row = norm_gain[None, :]
    cos, sin = (t[:, 0, :] for t in rope_tables(position, HD))
    key_rows, inv_tile = make_keys(hidden_in[0], full_weight, gain_row, cos, sin)
    (all_keys,) = exchange("dp", [key_rows], ["ag"], 2)

    slot_table = table[:, :, 0].reshape(-1)
    my_slots = here * blocks_dev + block_ids
    all_blocks = jnp.arange(slot_table.shape[0], dtype=jnp.int32)
    source_block = jnp.sum(
        jnp.where(slot_table[None, :] == my_slots[:, None], all_blocks[None, :], 0), axis=1
    )
    first_row = source_block * block_rows
    low = segment_starts(lengths, first_row)
    query_grad, kv_part = attend(
        source_block // blocks_dev,
        first_row,
        low,
        starts,
        incoming,
        all_keys.reshape(stream_len, key_width),
        all_values.reshape(stream_len, key_width),
    )
    (parts,) = exchange("dp", [kv_part.reshape(dp_size, row_count, 2 * key_width)], ["a2a"], 3)
    raw_grad, value_grad = make_raw(parts, cos, sin)
    raw_all, inv_all = exchange("shard", [raw_grad, inv_tile], ["ag", "ag"], 4)
    input_grad = own_rows(raw_grad, full_weight, hidden_in[0], inv_tile, gain_row)
    weight_grad, gain_grad = own_weight(z, raw_all, inv_all, key_weight, gain_row, pieces)
    return (
        input_grad[None],
        query_grad[None],
        value_grad[None],
        weight_grad[None],
        gain_grad,
    )


def solution(mesh):
    placed = (
        P("shard", "dp", None),
        P(),
        P("shard", None),
        P("shard", "dp", None),
        P("shard", "dp", None),
        P("shard", "dp", None),
        P("shard", "dp"),
        P("shard", "dp"),
        P("shard", None),
        P("shard", "dp"),
    )
    return jax.shard_map(
        local,
        mesh=mesh,
        in_specs=placed,
        out_specs=(
            P("shard", "dp", None),
            P("shard", "dp", None),
            P("shard", "dp", None),
            P("dp", "shard", None),
            P("dp", "shard"),
        ),
        check_vma=False,
    )
```

```python
import functools
import math

import jax
import jax.numpy as jnp
from jax import lax
from jax.experimental import pallas as pl
from jax.experimental.pallas import tpu as pltpu
from jax.sharding import PartitionSpec as P

HD = 128
QH = 32
KVH = 4
GROUPS = QH // KVH

norm_eps = 1e-05
rope_base = 500000.0
upper_log = math.log(1.2)
lower_log = math.log(0.8)
masked_score = -1e30
MESH = pl.DeviceIdType.MESH
F32 = jnp.float32
BF16 = jnp.bfloat16


def rope_tables(positions, head_size):
    half_size = head_size // 2
    frequency = rope_base ** (-(jnp.arange(half_size, dtype=F32) * 2.0) / head_size)
    angles = positions.astype(F32)[:, None] * frequency[None, :]
    return (jnp.cos(angles)[:, None, :], jnp.sin(angles)[:, None, :])


def segment_starts(lengths, row_ids):
    seg_ends = jnp.cumsum(lengths)
    starts = seg_ends - lengths
    inside = (row_ids[:, None] >= starts[None, :]) & (row_ids[:, None] < seg_ends[None, :])
    return jnp.sum(jnp.where(inside, starts[None, :], 0), axis=1)


def token_weight(advantage, ratio_log):
    keep_mask = jnp.where(advantage >= 0.0, ratio_log <= upper_log, ratio_log >= lower_log)
    return jnp.where(keep_mask, -advantage * jnp.exp(ratio_log), 0.0)


def exchange_kernel(axis, n, modes, with_weight, n_shard, *refs):
    count = len(modes)
    ins = refs[: count + with_weight]
    outs = refs[count + with_weight : 2 * (count + with_weight)]
    rest = refs[2 * (count + with_weight) :]
    send_sem, recv_sem, local_sem = rest[:3]
    me = lax.axis_index(axis)
    barrier = pltpu.get_barrier_semaphore()
    for k in range(1, n):
        pl.semaphore_signal(
            barrier, inc=1, device_id={axis: lax.rem(me + k, n)}, device_id_type=MESH
        )
    greeted = n - 1
    if with_weight:
        z = lax.axis_index("shard")
        for k in range(1, n_shard):
            pl.semaphore_signal(
                barrier, inc=1, device_id={"shard": lax.rem(z + k, n_shard)}, device_id_type=MESH
            )
        greeted += n_shard - 1
    pl.semaphore_wait(barrier, greeted)

    w_copies = []
    if with_weight:
        wsend, wrecv, fsend, frecv, nsend, nrecv, gsend, grecv, wloc = rest[3:]
        w_in, w_out = ins[count], outs[count]
        part_rows = w_in.shape[0] // 4
        core = lax.rem(me, 2)
        bit1 = lax.rem(lax.div(me, 2), 2)
        bit2 = lax.rem(lax.div(me, 4), 2)
        color = lax.rem(bit1 + bit2, 2)
        sibling = me + 1 - 2 * core
        neighbour = me + (1 - core) * (2 - 4 * bit1) + core * (4 - 8 * bit2)

        def part(index):
            return pl.ds(pl.multiple_of(index * part_rows, part_rows), part_rows)

        mine = part(2 * color + core)
        theirs = part(2 * (1 - color) + core)
        sib_mine = part(2 * color + 1 - core)
        sib_theirs = part(2 * (1 - color) + 1 - core)

        def over_z(k):
            return pltpu.make_async_remote_copy(
                src_ref=w_in.at[mine],
                dst_ref=w_out.at[z, mine],
                send_sem=wsend.at[k],
                recv_sem=wrecv.at[k],
                device_id={"shard": lax.rem(z + k, n_shard)},
                device_id_type=MESH,
            )

        def hand_on(source, rows, send, recv, k, target):
            return pltpu.make_async_remote_copy(
                src_ref=w_out.at[source, rows],
                dst_ref=w_out.at[source, rows],
                send_sem=send.at[k],
                recv_sem=recv.at[k],
                device_id={"dp": target},
                device_id_type=MESH,
            )

        for k in range(1, n_shard):
            c = over_z(k)
            c.start()
            w_copies.append(c)
    copies = []
    for a, mode in enumerate(modes):
        for k in range(1, n):
            peer = lax.rem(me + k, n)
            c = pltpu.make_async_remote_copy(
                src_ref=ins[a].at[peer] if mode == "a2a" else ins[a],
                dst_ref=outs[a].at[me],
                send_sem=send_sem.at[a, k],
                recv_sem=recv_sem.at[a, k],
                device_id={axis: peer},
                device_id_type=MESH,
            )
            c.start()
            copies.append(c)
    local_copies = []
    for a, mode in enumerate(modes):
        c = pltpu.make_async_copy(
            ins[a].at[me] if mode == "a2a" else ins[a], outs[a].at[me], local_sem.at[a]
        )
        c.start()
        local_copies.append(c)
    if with_weight:
        c = pltpu.make_async_copy(w_in, w_out.at[z], wloc)
        c.start()
        local_copies.append(c)
        sources = [lax.rem(z + n_shard - k, n_shard) for k in range(n_shard)]
        for k in range(1, n_shard):
            pltpu.make_async_remote_copy(
                src_ref=w_in.at[mine],
                dst_ref=w_out.at[sources[k], mine],
                send_sem=wsend.at[k],
                recv_sem=wrecv.at[k],
                device_id={"shard": lax.rem(z + k, n_shard)},
                device_id_type=MESH,
            ).wait_recv()
            for c in (
                hand_on(sources[k], mine, nsend, nrecv, k, neighbour),
                hand_on(sources[k], mine, fsend, frecv, k, sibling),
            ):
                c.start()
                w_copies.append(c)
        for k in range(1, n_shard):
            hand_on(sources[k], theirs, nsend, nrecv, k, neighbour).wait_recv()
            c = hand_on(sources[k], theirs, gsend, grecv, k, sibling)
            c.start()
            w_copies.append(c)
        for k in range(1, n_shard):
            hand_on(sources[k], sib_mine, fsend, frecv, k, sibling).wait_recv()
            hand_on(sources[k], sib_theirs, gsend, grecv, k, sibling).wait_recv()
        for c in w_copies:
            c.wait_send()
    for a, mode in enumerate(modes):
        for k in range(1, n):
            src = lax.rem(me + n - k, n)
            pltpu.make_async_remote_copy(
                src_ref=ins[a].at[src] if mode == "a2a" else ins[a],
                dst_ref=outs[a].at[src],
                send_sem=send_sem.at[a, k],
                recv_sem=recv_sem.at[a, k],
                device_id={axis: src},
                device_id_type=MESH,
            ).wait_recv()
    for c in copies:
        c.wait_send()
    for c in local_copies:
        c.wait()


def exchange(axis, arrays, modes, collective_id, weight=None):
    n = lax.axis_size(axis)
    n_shard = lax.axis_size("shard")
    outs = []
    for array, mode in zip(arrays, modes):
        block = array.shape[1:] if mode == "a2a" else array.shape
        outs.append(jax.ShapeDtypeStruct((n,) + block, array.dtype))
    sems = [
        pltpu.SemaphoreType.DMA((len(modes), n)),
        pltpu.SemaphoreType.DMA((len(modes), n)),
        pltpu.SemaphoreType.DMA((len(modes),)),
    ]
    operands = list(arrays)
    if weight is not None:
        operands.append(weight)
        outs.append(jax.ShapeDtypeStruct((n_shard,) + weight.shape, weight.dtype))
        sems += [pltpu.SemaphoreType.DMA((n_shard,))] * 8 + [pltpu.SemaphoreType.DMA]
    hbm = pl.BlockSpec(memory_space=pl.ANY)
    moved = sum(math.prod(o.shape) * o.dtype.itemsize for o in outs)
    return pl.pallas_call(
        functools.partial(
            exchange_kernel, axis, n, tuple(modes), int(weight is not None), n_shard
        ),
        out_shape=outs,
        in_specs=[hbm] * len(operands),
        out_specs=[hbm] * len(outs),
        scratch_shapes=sems,
        compiler_params=pltpu.CompilerParams(collective_id=collective_id, has_side_effects=True),
        cost_estimate=pl.CostEstimate(flops=0, bytes_accessed=20 * moved, transcendentals=0),
    )(*operands)


def pack_kernel(pick_ref, q_ref, g_ref, w_ref, out_ref):
    width = q_ref.shape[1]
    out_ref[0, :, :width] = q_ref[...]
    out_ref[0, :, width:] = (w_ref[...] * g_ref[...].astype(F32)).astype(BF16)


def pack_rows(pick, queries, logp, weight_col, block_rows, dp_size):
    width = queries.shape[1]
    return pl.pallas_call(
        pack_kernel,
        out_shape=jax.ShapeDtypeStruct((dp_size, block_rows, 2 * width), BF16),
        grid_spec=pltpu.PrefetchScalarGridSpec(
            num_scalar_prefetch=1,
            grid=(dp_size,),
            in_specs=[
                pl.BlockSpec((block_rows, width), lambda d, p: (p[d], 0)),
                pl.BlockSpec((block_rows, width), lambda d, p: (p[d], 0)),
                pl.BlockSpec((block_rows, 1), lambda d, p: (p[d], 0)),
            ],
            out_specs=pl.BlockSpec((1, block_rows, 2 * width), lambda d, p: (d, 0, 0)),
        ),
        cost_estimate=pl.CostEstimate(
            flops=0, bytes_accessed=8 * dp_size * block_rows * width, transcendentals=0
        ),
    )(pick, queries, logp, weight_col)


def dot_nt(a, b):
    return lax.dot_general(a, b, (((1,), (1,)), ((), ())), preferred_element_type=F32)


def dot_tn(a, b):
    return lax.dot_general(a, b, (((0,), (0,)), ((), ())), preferred_element_type=F32)


def attend_kernel(windows, src_ref, row_ref, low_ref, starts_ref, x_ref, k_ref, v_ref, qg_ref, kv_ref, dk, dv):
    slot = pl.program_id(0)
    stream_len = dk.shape[0]
    block_rows = x_ref.shape[1]
    half = QH * HD
    scale = 1.0 / math.sqrt(HD)
    first_row = row_ref[slot]
    low = (low_ref[slot] // 128) * 128
    span = first_row + block_rows - low

    @pl.when(slot == 0)
    def _():
        dk[...] = jnp.zeros_like(dk)
        dv[...] = jnp.zeros_like(dv)

    m_rows = GROUPS * block_rows
    pos = first_row + lax.rem(lax.broadcasted_iota(jnp.int32, (m_rows, 1), 0), block_rows)
    seg_low = jnp.zeros_like(pos)
    for r in range(1, starts_ref.shape[0]):
        seg_low = jnp.where(pos >= starts_ref[r], starts_ref[r], seg_low)

    def body(width):
        start = pl.multiple_of(jnp.minimum(low, stream_len - width), 128)
        j = start + lax.broadcasted_iota(jnp.int32, (m_rows, width), 1)
        allowed = (j >= seg_low) & (j <= pos)
        rows = pl.ds(start, width)
        for h in range(KVH):
            cols = slice(h * HD, (h + 1) * HD)
            base = h * GROUPS * HD
            q = jnp.concatenate(
                [x_ref[0, :, base + g * HD : base + (g + 1) * HD] for g in range(GROUPS)], axis=0
            )
            og = jnp.concatenate(
                [
                    x_ref[0, :, half + base + g * HD : half + base + (g + 1) * HD]
                    for g in range(GROUPS)
                ],
                axis=0,
            )
            k = k_ref[rows, cols]
            v = v_ref[rows, cols]
            s = jnp.where(allowed, dot_nt(q, k) * scale, masked_score)
            e = jnp.exp(s - jnp.max(s, axis=1, keepdims=True))
            p = e * (1.0 / jnp.sum(e, axis=1, keepdims=True))
            pb = p.astype(BF16)
            dp = dot_nt(og, v)
            delta = jnp.sum(pb.astype(F32) * dp, axis=1, keepdims=True)
            ds = (p * (dp - delta)).astype(BF16)
            dq = (jnp.dot(ds, k, preferred_element_type=F32) * scale).astype(BF16)
            for g in range(GROUPS):
                qg_ref[:, base + g * HD : base + (g + 1) * HD] = dq[
                    g * block_rows : (g + 1) * block_rows
                ]
            dk[rows, cols] += dot_tn(ds, q)
            dv[rows, cols] += dot_tn(pb, og)

    before = 0
    for width in windows:
        last = width == windows[-1]
        fits = (span > before) if last else (span > before) & (span <= width)

        @pl.when(fits)
        def _(width=width):
            body(width)

        before = width

    @pl.when(slot == pl.num_programs(0) - 1)
    def _():
        kw = dk.shape[1]
        kv_ref[:, :kw] = (dk[...] * scale).astype(BF16)
        kv_ref[:, kw:] = dv[...].astype(BF16)


def attend(src, first_row, low, starts, incoming, keys, values):
    stream_len, kw = keys.shape
    slots = src.shape[0]
    block_rows = incoming.shape[1]
    windows = tuple(w for w in (128, 256, 384, 512, 640, 768) if w < stream_len) + (stream_len,)
    whole = lambda s, *_: (0, 0)
    return pl.pallas_call(
        functools.partial(attend_kernel, windows),
        out_shape=[
            jax.ShapeDtypeStruct((slots * block_rows, QH * HD), BF16),
            jax.ShapeDtypeStruct((stream_len, 2 * kw), BF16),
        ],
        grid_spec=pltpu.PrefetchScalarGridSpec(
            num_scalar_prefetch=4,
            grid=(slots,),
            in_specs=[
                pl.BlockSpec((1, block_rows, incoming.shape[2]), lambda s, a, *_: (a[s], 0, 0)),
                pl.BlockSpec((stream_len, kw), whole),
                pl.BlockSpec((stream_len, kw), whole),
            ],
            out_specs=[
                pl.BlockSpec((block_rows, QH * HD), lambda s, *_: (s, 0)),
                pl.BlockSpec((stream_len, 2 * kw), whole),
            ],
            scratch_shapes=[pltpu.VMEM((stream_len, kw), F32), pltpu.VMEM((stream_len, kw), F32)],
        ),
        compiler_params=pltpu.CompilerParams(vmem_limit_bytes=48 * 1024 * 1024),
        cost_estimate=pl.CostEstimate(
            flops=20_000_000_000, bytes_accessed=60_000_000, transcendentals=4_000_000
        ),
    )(src, first_row, low, starts, incoming, keys, values)


def keys_kernel(x_ref, w_ref, gain_ref, cos_ref, sin_ref, key_ref, inv_ref, acc, inv):
    step = pl.program_id(0)
    chunk = w_ref.shape[0]
    width = x_ref.shape[1]

    @pl.when(step == 0)
    def _():
        total = jnp.zeros((x_ref.shape[0], 1), F32)
        for c in range(0, width, 1024):
            x = x_ref[:, c : c + 1024].astype(F32)
            total += jnp.sum(x * x, axis=1, keepdims=True)
        inv[...] = lax.rsqrt(total / width + norm_eps)
        inv_ref[...] = jnp.broadcast_to(inv[...], inv_ref.shape)
        acc[...] = jnp.zeros_like(acc)

    cols = pl.ds(pl.multiple_of(step * chunk, chunk), chunk)
    normed = x_ref[:, cols].astype(F32) * inv[...]
    normed_in = (normed * gain_ref[:, cols].astype(F32)).astype(BF16)
    acc[...] += jnp.dot(normed_in, w_ref[...], preferred_element_type=F32)

    @pl.when(step == pl.num_programs(0) - 1)
    def _():
        half = HD // 2
        cos, sin = cos_ref[...], sin_ref[...]
        for h in range(KVH):
            a = acc[:, h * HD : h * HD + half]
            b = acc[:, h * HD + half : (h + 1) * HD]
            key_ref[:, h * HD : (h + 1) * HD] = jnp.concatenate(
                [a * cos - b * sin, b * cos + a * sin], axis=1
            ).astype(BF16)


def make_keys(x, weight, gain, cos, sin):
    rows, width = x.shape
    kw = weight.shape[1]
    chunk = 1024
    whole = lambda c: (0, 0)
    return pl.pallas_call(
        keys_kernel,
        out_shape=[
            jax.ShapeDtypeStruct((rows, kw), BF16),
            jax.ShapeDtypeStruct((rows, 128), F32),
        ],
        grid=(width // chunk,),
        in_specs=[
            pl.BlockSpec((rows, width), whole),
            pl.BlockSpec((chunk, kw), lambda c: (c, 0)),
            pl.BlockSpec((1, width), whole),
            pl.BlockSpec(cos.shape, whole),
            pl.BlockSpec(sin.shape, whole),
        ],
        out_specs=[pl.BlockSpec((rows, kw), whole), pl.BlockSpec((rows, 128), whole)],
        scratch_shapes=[pltpu.VMEM((rows, kw), F32), pltpu.VMEM((rows, 1), F32)],
        compiler_params=pltpu.CompilerParams(vmem_limit_bytes=40 * 1024 * 1024),
        cost_estimate=pl.CostEstimate(
            flops=2 * rows * width * kw, bytes_accessed=4 * width * kw, transcendentals=0
        ),
    )(x, weight, gain, cos, sin)


def raw_kernel(parts_ref, cos_ref, sin_ref, raw_ref, value_ref):
    kw = raw_ref.shape[1]
    half = HD // 2
    total = parts_ref[0].astype(F32)
    for i in range(1, parts_ref.shape[0]):
        total += parts_ref[i].astype(F32)
    value_ref[...] = total[:, kw:].astype(BF16)
    cos, sin = cos_ref[...], sin_ref[...]
    for h in range(KVH):
        a = total[:, h * HD : h * HD + half]
        b = total[:, h * HD + half : (h + 1) * HD]
        raw_ref[:, h * HD : (h + 1) * HD] = jnp.concatenate(
            [a * cos + b * sin, b * cos - a * sin], axis=1
        ).astype(BF16)


def make_raw(parts, cos, sin):
    rows = parts.shape[1]
    kw = parts.shape[2] // 2
    return pl.pallas_call(
        raw_kernel,
        out_shape=[jax.ShapeDtypeStruct((rows, kw), BF16)] * 2,
        compiler_params=pltpu.CompilerParams(vmem_limit_bytes=40 * 1024 * 1024),
    )(parts, cos, sin)


def rows_kernel(raw_ref, w_ref, x_ref, inv_ref, gain_ref, out_ref, grads, total):
    step = pl.program_id(0)
    chunk = w_ref.shape[0]
    width = x_ref.shape[1]
    inv = inv_ref[:, :1]

    @pl.when(step == 0)
    def _():
        total[...] = jnp.zeros_like(total)

    cols = pl.ds(pl.multiple_of(step * chunk, chunk), chunk)
    grad = dot_nt(raw_ref[...], w_ref[...]).astype(BF16)
    grads[:, cols] = grad
    scaled = grad.astype(F32) * gain_ref[:, cols].astype(F32)
    normed = x_ref[:, cols].astype(F32) * inv
    total[...] += jnp.sum(scaled * normed, axis=1, keepdims=True)

    @pl.when(step == pl.num_programs(0) - 1)
    def _():
        mean = total[...] / width
        for c in range(0, width, 1024):
            part = slice(c, c + 1024)
            scaled = grads[:, part].astype(F32) * gain_ref[:, part].astype(F32)
            normed = x_ref[:, part].astype(F32) * inv
            out_ref[:, part] = (inv * (scaled - normed * mean)).astype(BF16)


def own_rows(raw, weight, x, inv, gain):
    rows, width = x.shape
    kw = weight.shape[1]
    chunk = 1024
    whole = lambda c: (0, 0)
    return pl.pallas_call(
        rows_kernel,
        out_shape=jax.ShapeDtypeStruct((rows, width), BF16),
        grid=(width // chunk,),
        in_specs=[
            pl.BlockSpec((rows, kw), whole),
            pl.BlockSpec((chunk, kw), lambda c: (c, 0)),
            pl.BlockSpec((rows, width), whole),
            pl.BlockSpec((rows, 128), whole),
            pl.BlockSpec((1, width), whole),
        ],
        out_specs=pl.BlockSpec((rows, width), whole),
        scratch_shapes=[pltpu.VMEM((rows, width), BF16), pltpu.VMEM((rows, 1), F32)],
        compiler_params=pltpu.CompilerParams(vmem_limit_bytes=40 * 1024 * 1024),
        cost_estimate=pl.CostEstimate(
            flops=2 * rows * width * kw, bytes_accessed=4 * width * kw, transcendentals=0
        ),
    )(raw, weight, x, inv, gain)


def to_all_shards(array):
    n = lax.axis_size("shard")
    return [array] + [
        lax.ppermute(array, "shard", [(i, (i + k) % n) for i in range(n)]) for k in range(1, n)
    ]


def own_kernel(n, z_ref, w_ref, gain_ref, *refs):
    raws, invs, pieces, (wg_ref, gg_ref) = refs[:n], refs[n : 2 * n], refs[2 * n : 3 * n], refs[3 * n :]
    gain = gain_ref[...].astype(F32)
    weight = w_ref[...]
    weight_sum = None
    for k in range(n):
        raw = raws[k][...]
        inv = invs[k][:, :1]
        normed = pieces[k][...].astype(F32) * inv
        term = dot_tn((normed * gain).astype(BF16), raw).astype(BF16).astype(F32)
        grad = dot_nt(raw, weight).astype(BF16).astype(F32)
        row = jnp.sum(grad * normed, axis=0, keepdims=True).astype(BF16).astype(F32)
        weight_sum = term if k == 0 else weight_sum + term
        gain_sum = row if k == 0 else gain_sum + row
    wg_ref[...] = weight_sum
    gg_ref[...] = gain_sum


def own_weight(z, raw_all, inv_all, weight, gain, pieces):
    n = len(raw_all)
    rows, kw = raw_all[0].shape
    slice_w = weight.shape[0]
    chunk = min(256, slice_w)
    steps = slice_w // chunk
    whole = lambda c, zr: (0, 0)
    return pl.pallas_call(
        functools.partial(own_kernel, n),
        out_shape=[
            jax.ShapeDtypeStruct((slice_w, kw), F32),
            jax.ShapeDtypeStruct((1, slice_w), F32),
        ],
        grid_spec=pltpu.PrefetchScalarGridSpec(
            num_scalar_prefetch=1,
            grid=(steps,),
            in_specs=[
                pl.BlockSpec((chunk, kw), lambda c, zr: (c, 0)),
                pl.BlockSpec((1, chunk), lambda c, zr: (0, zr[0] * steps + c)),
            ]
            + [pl.BlockSpec((rows, kw), whole)] * n
            + [pl.BlockSpec(inv_all[0].shape, whole)] * n
            + [pl.BlockSpec((rows, chunk), lambda c, zr: (0, c))] * n,
            out_specs=[
                pl.BlockSpec((chunk, kw), lambda c, zr: (c, 0)),
                pl.BlockSpec((1, chunk), lambda c, zr: (0, c)),
            ],
        ),
        compiler_params=pltpu.CompilerParams(vmem_limit_bytes=40 * 1024 * 1024),
        cost_estimate=pl.CostEstimate(
            flops=4 * n * rows * slice_w * kw, bytes_accessed=12 * slice_w * kw, transcendentals=0
        ),
    )(z.reshape(1), weight, gain, *raw_all, *inv_all, *pieces)


def local(
    hidden_in,
    norm_gain,
    key_weight,
    queries,
    logp_grad,
    values,
    advantages,
    log_ratio,
    resp_lengths,
    block_slots,
):
    row_count, width = hidden_in.shape[1:]
    dp_size = lax.axis_size("dp")
    n_shard = lax.axis_size("shard")
    stream_len = row_count * dp_size
    blocks_dev = block_slots.shape[1]
    block_rows = row_count // blocks_dev
    slice_w, key_width = key_weight.shape
    here = lax.axis_index("dp")
    z = lax.axis_index("shard")
    row_ids = here * row_count + jnp.arange(row_count, dtype=jnp.int32)
    lengths = resp_lengths[0]
    starts = jnp.cumsum(lengths) - lengths
    position = row_ids - segment_starts(lengths, row_ids)

    slot_list = block_slots[0]
    dest_dev = slot_list // blocks_dev
    block_ids = jnp.arange(blocks_dev, dtype=jnp.int32)
    dev_ids = jnp.arange(dp_size, dtype=jnp.int32)
    pick = jnp.sum(jnp.where(dest_dev[None, :] == dev_ids[:, None], block_ids[None, :], 0), axis=1)
    weight_tok = token_weight(advantages[0], log_ratio[0])
    outgoing = pack_rows(
        pick, queries[0], logp_grad[0], weight_tok[:, None], block_rows, dp_size
    )
    slot_tile = jnp.broadcast_to(slot_list[:, None], (blocks_dev, 128))
    incoming = lax.all_to_all(outgoing, "dp", split_axis=0, concat_axis=0, tiled=True)
    table, all_values, full_weight = exchange(
        "dp", [slot_tile, values[0]], ["ag", "ag"], 1, weight=key_weight
    )
    full_weight = full_weight.reshape(width, key_width)

    pieces = []
    for k in range(n_shard):
        target = lax.rem(z + k, n_shard)
        pieces.append(lax.dynamic_slice_in_dim(hidden_in[0], target * slice_w, slice_w, 1))
    pieces, full_weight = lax.optimization_barrier((pieces, full_weight))
    for k in range(1, n_shard):
        pieces[k] = lax.ppermute(
            pieces[k], "shard", [(i, (i + k) % n_shard) for i in range(n_shard)]
        )

    gain_row = norm_gain[None, :]
    cos, sin = (t[:, 0, :] for t in rope_tables(position, HD))
    key_rows, inv_tile = make_keys(hidden_in[0], full_weight, gain_row, cos, sin)
    inv_all = to_all_shards(inv_tile)
    (all_keys,) = exchange("dp", [key_rows], ["ag"], 2)

    slot_table = table[:, :, 0].reshape(-1)
    my_slots = here * blocks_dev + block_ids
    all_blocks = jnp.arange(slot_table.shape[0], dtype=jnp.int32)
    source_block = jnp.sum(
        jnp.where(slot_table[None, :] == my_slots[:, None], all_blocks[None, :], 0), axis=1
    )
    first_row = source_block * block_rows
    low = segment_starts(lengths, first_row)
    query_grad, kv_part = attend(
        source_block // blocks_dev,
        first_row,
        low,
        starts,
        incoming,
        all_keys.reshape(stream_len, key_width),
        all_values.reshape(stream_len, key_width),
    )
    (parts,) = exchange("dp", [kv_part.reshape(dp_size, row_count, 2 * key_width)], ["a2a"], 3)
    raw_grad, value_grad = make_raw(parts, cos, sin)
    raw_all = to_all_shards(raw_grad)
    input_grad = own_rows(raw_grad, full_weight, hidden_in[0], inv_tile, gain_row)
    weight_grad, gain_grad = own_weight(z, raw_all, inv_all, key_weight, gain_row, pieces)
    return (
        input_grad[None],
        query_grad[None],
        value_grad[None],
        weight_grad[None],
        gain_grad,
    )


def solution(mesh):
    placed = (
        P("shard", "dp", None),
        P(),
        P("shard", None),
        P("shard", "dp", None),
        P("shard", "dp", None),
        P("shard", "dp", None),
        P("shard", "dp"),
        P("shard", "dp"),
        P("shard", None),
        P("shard", "dp"),
    )
    return jax.shard_map(
        local,
        mesh=mesh,
        in_specs=placed,
        out_specs=(
            P("shard", "dp", None),
            P("shard", "dp", None),
            P("shard", "dp", None),
            P("dp", "shard", None),
            P("dp", "shard"),
        ),
        check_vma=False,
    )
```
